128 devices in a mesh: row: 16 (over x, y), col: 8 (over z, core).
Axes of the slice: x: 4, y: 4, z: 4, core: 2. Of those that a mesh axis runs over, the one named last changes fastest.
Arguments:
- features: float32 [384, 768, 256], P('row', 'col'), may hold values from -6 to 6
- depth_kernel: float32 [3, 3, 256], replicated, may hold values from -1.5 to 1.5
- value_weight: float32 [256, 256], replicated, may hold values from -0.375 to 0.375
- key_weight: float32 [256, 256], replicated, may hold values from -0.375 to 0.375
- centers: float32 [512, 256], replicated, may hold values from -6 to 6
- center_gain: float32 [256], replicated, may hold values from 0.1 to 1.9
- labels: int32 [384, 768], P('row', 'col'), may hold values from 0 to 511
- cotangent: float32 [384, 768, 512], P('row', 'col'), may hold values from -6 to 6
Outputs:
- new_centers: float32 [512, 256], replicated
- logits: float32 [384, 768, 512], P('row', 'col')
- grad_features: float32 [384, 768, 256], P('row', 'col')
- grad_centers: float32 [512, 256], replicated
- grad_value: float32 [256, 256], replicated
- grad_key: float32 [256, 256], replicated
The draws below stay inside these ranges and needn't reach their ends.
All inputs are finite; a program needn't handle non-finite values.
Results may differ from the reference program's by a relative error of at most 0.00011.
Values sent between devices are 32-bit elements; how exact they have to be, the bound alone decides.
A program may use at most 64 MiB of HBM per device.

```python
import jax
import jax.numpy as jnp
from jax import lax

D = 256
K = 512
HT = 24
WT = 96
NH = 384
NW = 768


def draw_labels(key, part):
    key = jax.random.fold_in(key, 7)
    first, second, third = jax.random.split(key, 3)
    tiles_across = NW // WT
    tile = (jnp.arange(NH, dtype=jnp.int32) // HT)[:, None] * tiles_across + (jnp.arange(NW, dtype=jnp.int32) // WT)[None, :]
    per_tile = K // (NH // HT * tiles_across)
    home = tile * per_tile + jax.random.randint(first, (NH, NW), 0, per_tile)
    anywhere = jax.random.randint(second, (NH, NW), 0, K)
    picker = jax.random.randint(third, (NH, NW), 0, 4)
    return jnp.where(picker == 0, anywhere, home).astype(jnp.int32)


def strengthened(drawn, stream_key, source, target, blocks, factor):
    def block_of(axis_at):
        return (jnp.arange(drawn.shape[axis_at]) // (drawn.shape[axis_at] // blocks)).reshape((-1,) + (1,) * (drawn.ndim - 1 - axis_at))

    near = jax.random.permutation(stream_key, blocks)[block_of(target)]
    second = (block_of(target) + blocks // 2) % blocks
    return jnp.where((block_of(source) == near) | (block_of(source) == second), factor * drawn, drawn)


def levels(rng, extent, pieces, smallest, largest):
    level = 1.0
    for axis_at, blocks in pieces:
        draws = jax.random.uniform(jax.random.fold_in(jax.random.fold_in(rng, 6), axis_at), (blocks,), jnp.float32, smallest / len(pieces), largest / len(pieces))
        level = level * jnp.repeat(jnp.exp(draws), extent[axis_at] // blocks).reshape((-1,) + (1,) * (len(extent) - 1 - axis_at))
    return level


def scatter_about(rng, dims, deviation, bound, shards=(), kind=jnp.bfloat16):
    gain = levels(rng, dims, shards, -0.22, 0.18) if shards else 1.0
    drawn = jax.random.normal(rng, dims, jnp.float32) * deviation * gain
    return jnp.minimum(jnp.maximum(drawn, -bound), bound).astype(kind)


def heavy_noise(stream_key, extent, width, most, cuts, heavy, kind=jnp.bfloat16):
    values = width * jax.random.normal(stream_key, extent, jnp.float32)
    if cuts:
        values = values * levels(stream_key, extent, cuts, -0.22, 0.18)
    return jnp.clip(strengthened(values, jax.random.fold_in(stream_key, 3), *heavy), -most, most).astype(kind)


def setup_inputs(seed: int = 0) -> dict:
    streams_of = jax.random.split(jax.random.key(seed), 9)
    features = scatter_about(streams_of[0], (NH, NW, D), 1.0, 6.0, ((0, 16), (1, 8)), jnp.float32)
    depth_kernel = scatter_about(streams_of[1], (3, 3, D), 0.3, 1.5, (), jnp.float32)
    value_weight = scatter_about(streams_of[2], (D, D), D ** -0.5, 0.375, (), jnp.float32)
    key_weight = scatter_about(streams_of[3], (D, D), D ** -0.5, 0.375, (), jnp.float32)
    centers = scatter_about(streams_of[4], (K, D), 1.0, 6.0, (), jnp.float32)
    center_gain = jnp.clip(1.0 + 0.18 * jax.random.normal(streams_of[5], (D,), jnp.float32), 0.1, 1.9)
    labels = draw_labels(jax.random.fold_in(streams_of[8], 71), 0)
    cotangent = heavy_noise(streams_of[7], (NH, NW, K), 1.0, 6.0, ((0, 16), (1, 8)), (0, 2, 16, 2.0), jnp.float32)
    return dict(features=features, depth_kernel=depth_kernel, value_weight=value_weight, key_weight=key_weight, centers=centers, center_gain=center_gain, labels=labels, cotangent=cotangent)


def mix_grid(field, kernel):
    rows, cols = (field.shape[0], field.shape[1])
    padded = jnp.pad(field, ((1, 1), (1, 1), (0, 0)))
    result = field
    for a in range(3):
        for b in range(3):
            result = result + kernel[a, b] * padded[a:a + rows, b:b + cols]
    return result

def unmix_grid(field, kernel):
    rows, cols = (field.shape[0], field.shape[1])
    padded = jnp.pad(field, ((1, 1), (1, 1), (0, 0)))
    result = field
    for a in range(3):
        for b in range(3):
            result = result + kernel[a, b] * padded[2 - a:2 - a + rows, 2 - b:2 - b + cols]
    return result

def matmul(left, right):
    return jnp.dot(left, right, preferred_element_type=jnp.float32, precision=lax.Precision.HIGHEST)

def reference(features, depth_kernel, value_weight, key_weight, centers, center_gain, labels, cotangent):
    chans = features.shape[2]
    count = centers.shape[0]
    scale = 1.0 / jnp.sqrt(jnp.float32(chans))
    mixed = mix_grid(features, depth_kernel).reshape(-1, chans)
    values = matmul(mixed, value_weight)
    keys = matmul(mixed, key_weight)
    flat_labels = labels.reshape(-1).astype(jnp.int32)
    sums = jax.ops.segment_sum(values, flat_labels, num_segments=count)
    centred = sums - lax.optimization_barrier(jnp.mean(sums, axis=1, keepdims=True))
    inverse = lax.rsqrt(lax.optimization_barrier(jnp.mean(centred * centred, axis=1, keepdims=True)) + 1e-05)
    normed = centred * inverse
    new_centers = centers + center_gain * normed
    logits = matmul(keys, new_centers.T) * scale
    grads = cotangent.reshape(-1, count)
    grad_centers = matmul(grads.T, keys) * scale
    dkeys = matmul(grads, new_centers) * scale
    dnorm = grad_centers * center_gain
    dsums = inverse * (dnorm - lax.optimization_barrier(jnp.mean(dnorm, axis=1, keepdims=True)) - normed * lax.optimization_barrier(jnp.mean(dnorm * normed, axis=1, keepdims=True)))
    dvalues = dsums[flat_labels]
    grad_value = matmul(mixed.T, dvalues)
    grad_key = matmul(mixed.T, dkeys)
    dmixed = matmul(dvalues, value_weight.T) + matmul(dkeys, key_weight.T)
    grad_features = unmix_grid(dmixed.reshape(features.shape), depth_kernel)
    return (new_centers, logits.reshape(features.shape[0], features.shape[1], count), grad_features, grad_centers, grad_value, grad_key)
```

```python
import jax
import jax.numpy as jnp
from jax import lax
from jax.sharding import PartitionSpec as P


def padded_2(cells, sides, width):
    for axis, dim in sides:
        count = lax.axis_size(axis)
        ends = count - 1
        head = lax.slice_in_dim(cells, 0, width, axis=dim)
        tail = lax.slice_in_dim(cells, cells.shape[dim] - width, cells.shape[dim], axis=dim)
        cells = jnp.concatenate(
            [
                lax.ppermute(tail, axis, [(i, (i + 1) % count) for i in range(ends)]),
                cells,
                lax.ppermute(head, axis, [((i + 1) % count, i) for i in range(ends)]),
            ],
            axis=dim,
        )
    return cells


def matmul(left, right):
    return jnp.dot(left, right, preferred_element_type=jnp.float32, precision=lax.Precision.HIGHEST)


def inner_rows(left, right):
    return lax.dot_general(
        left,
        right,
        (((0,), (0,)), ((), ())),
        preferred_element_type=jnp.float32,
        precision=lax.Precision.HIGHEST,
    )


def normalize(sums):
    centred = sums - jnp.mean(sums, axis=1, keepdims=True)
    inverse = lax.rsqrt(jnp.mean(centred * centred, axis=1, keepdims=True) + 1e-05)
    return (centred * inverse, inverse)


def shards(
    features, depth_kernel, value_weight, key_weight, centers, center_gain, labels, cotangent
):
    rows, cols, chans = features.shape
    count = centers.shape[0]
    scale = 1.0 / jnp.sqrt(jnp.float32(chans))
    padded = padded_2(features, (("row", 0), ("col", 1)), 1)
    mixed = features
    for a in range(3):
        for b in range(3):
            mixed = mixed + depth_kernel[a, b] * padded[a : a + rows, b : b + cols]
    mixed = mixed.reshape(-1, chans)
    onehot = (labels.reshape(-1)[:, None] == lax.iota(jnp.int32, count)[None, :]).astype(
        jnp.float32
    )
    grads = cotangent.reshape(-1, count)
    by_label = inner_rows(onehot, mixed)
    by_grad = inner_rows(grads, mixed)
    by_label, by_grad = lax.psum((by_label, by_grad), ("row", "col"))
    sums = matmul(by_label, value_weight)
    normed, inverse = normalize(sums)
    new_centers = centers + center_gain * normed
    back = matmul(new_centers, key_weight.T) * scale
    logits = matmul(mixed, back.T)
    grad_centers = matmul(by_grad, key_weight) * scale
    grad_key = inner_rows(by_grad, new_centers) * scale
    dnorm = grad_centers * center_gain
    dsums = inverse * (
        dnorm
        - jnp.mean(dnorm, axis=1, keepdims=True)
        - normed * jnp.mean(dnorm * normed, axis=1, keepdims=True)
    )
    grad_value = inner_rows(by_label, dsums)
    dmixed = (matmul(onehot, matmul(dsums, value_weight.T)) + matmul(grads, back)).reshape(
        rows, cols, chans
    )
    rim = padded_2(dmixed, (("row", 0), ("col", 1)), 1)
    grad_features = dmixed
    for a in range(3):
        for b in range(3):
            grad_features = (
                grad_features + depth_kernel[a, b] * rim[2 - a : 2 - a + rows, 2 - b : 2 - b + cols]
            )
    return (
        new_centers,
        logits.reshape(rows, cols, count),
        grad_features,
        grad_centers,
        grad_value,
        grad_key,
    )


def solution(mesh):
    return jax.shard_map(
        shards,
        mesh=mesh,
        in_specs=(
            P("row", "col", None),
            P(),
            P(),
            P(),
            P(),
            P(),
            P("row", "col"),
            P("row", "col", None),
        ),
        out_specs=(P(), P("row", "col", None), P("row", "col", None), P(), P(), P()),
        check_vma=False,
    )
```

```python
import jax
import jax.numpy as jnp
from jax import lax
from jax.experimental import pallas as pl
from jax.experimental.pallas import tpu as pltpu
from jax.sharding import PartitionSpec as P

MESH = pl.DeviceIdType.MESH


def place():
    r, c = lax.axis_index("row"), lax.axis_index("col")
    return r // 4, lax.rem(r, 4), c // 2, lax.rem(c, 2)


def at(x, y, z, k):
    return (lax.rem(x, 4) * 4 + lax.rem(y, 4), lax.rem(z, 4) * 2 + k)


def chip_at(t):
    x, y, z, k = place()
    x, y, z = x + t // 16 + 2, y + lax.rem(t // 4, 4) + 2, z + lax.rem(t, 4) + 2
    x, y, z = lax.rem(x, 4), lax.rem(y, 4), lax.rem(z, 4)
    return (x * 4 + y, z * 2 + k), x * 16 + y * 4 + z


SELF = 42


def signal(sem, device):
    pl.semaphore_signal(sem, inc=1, device_id=device, device_id_type=MESH)


def remote(src, dst, send, recv, device):
    return pltpu.make_async_remote_copy(
        src_ref=src, dst_ref=dst, send_sem=send, recv_sem=recv, device_id=device, device_id_type=MESH
    )


def others(step):
    lax.fori_loop(0, SELF, lambda t, _: step(t, t), None)
    lax.fori_loop(SELF + 1, 64, lambda t, _: step(t, t - 1), None)


def all_reduce_kernel(parts, out, partner_part, chip_sum, landing, met, sems):
    x, y, z, k = place()
    me = x * 16 + y * 4 + z
    lines = (
        [at(x + d, y, z, k) for d in (1, 2, 3)],
        [at(x, y + d, z, k) for d in (1, 2, 3)],
        [at(x, y, z + d, k) for d in (1, 2, 3)],
    )
    partner = at(x, y, z, 1 - k)
    barrier = pltpu.get_barrier_semaphore()
    for device in [*lines[0], *lines[1], *lines[2], partner]:
        signal(barrier, device)
    pl.semaphore_wait(barrier, 10)
    pair = remote(parts.at[1 - k], partner_part, sems.at[0], sems.at[1], partner)
    pair.start()
    for stage in range(2):
        for device in lines[stage]:
            signal(met.at[stage], device)
        pl.semaphore_wait(met.at[stage], 3)
    pair.wait()
    chip_sum[...] = parts[k] + partner_part[...]

    def scatter(t, slot):
        device, chip = chip_at(t)
        remote(chip_sum.at[chip], landing.at[slot], sems.at[2], sems.at[3], device).start()

    others(scatter)
    pltpu.make_async_copy(landing, landing, sems.at[3]).wait()
    out[k, me] = chip_sum[me] + jnp.sum(landing[...], axis=0)

    def gather(t, slot):
        device, _ = chip_at(t)
        remote(out.at[k, me], out.at[k, me], sems.at[4], sems.at[5], device).start()

    others(gather)
    pltpu.make_async_copy(landing, landing, sems.at[5]).wait()
    back = remote(out.at[k], out.at[k], sems.at[6], sems.at[7], partner)
    back.start()
    pltpu.make_async_copy(landing, landing, sems.at[2]).wait()
    pltpu.make_async_copy(landing, landing, sems.at[4]).wait()
    back.wait()


def all_reduce(parts):
    tile = (64, 8, 256)
    whole = pl.BlockSpec(memory_space=pltpu.VMEM)
    return pl.pallas_call(
        all_reduce_kernel,
        out_shape=jax.ShapeDtypeStruct((2, *tile), jnp.float32),
        in_specs=[whole],
        out_specs=whole,
        scratch_shapes=[
            pltpu.VMEM(tile, jnp.float32),
            pltpu.VMEM(tile, jnp.float32),
            pltpu.VMEM((63, 8, 256), jnp.float32),
            pltpu.SemaphoreType.REGULAR((2,)),
            pltpu.SemaphoreType.DMA((8,)),
        ],
        compiler_params=pltpu.CompilerParams(collective_id=0, has_side_effects=True),
    )(parts)


def padded_2(cells, sides, width):
    for axis, dim in sides:
        count = lax.axis_size(axis)
        ends = count - 1
        head = lax.slice_in_dim(cells, 0, width, axis=dim)
        tail = lax.slice_in_dim(cells, cells.shape[dim] - width, cells.shape[dim], axis=dim)
        cells = jnp.concatenate(
            [
                lax.ppermute(tail, axis, [(i, (i + 1) % count) for i in range(ends)]),
                cells,
                lax.ppermute(head, axis, [((i + 1) % count, i) for i in range(ends)]),
            ],
            axis=dim,
        )
    return cells


def matmul(left, right):
    return jnp.dot(left, right, preferred_element_type=jnp.float32, precision=lax.Precision.HIGHEST)


def inner_rows(left, right):
    return lax.dot_general(
        left,
        right,
        (((0,), (0,)), ((), ())),
        preferred_element_type=jnp.float32,
        precision=lax.Precision.HIGHEST,
    )


def normalize(sums):
    centred = sums - jnp.mean(sums, axis=1, keepdims=True)
    inverse = lax.rsqrt(jnp.mean(centred * centred, axis=1, keepdims=True) + 1e-05)
    return (centred * inverse, inverse)


def shards(
    features, depth_kernel, value_weight, key_weight, centers, center_gain, labels, cotangent
):
    rows, cols, chans = features.shape
    count = centers.shape[0]
    scale = 1.0 / jnp.sqrt(jnp.float32(chans))
    padded = padded_2(features, (("row", 0), ("col", 1)), 1)
    mixed = features
    for a in range(3):
        for b in range(3):
            mixed = mixed + depth_kernel[a, b] * padded[a : a + rows, b : b + cols]
    mixed = mixed.reshape(-1, chans)
    onehot = (labels.reshape(-1)[:, None] == lax.iota(jnp.int32, count)[None, :]).astype(
        jnp.float32
    )
    grads = cotangent.reshape(-1, count)
    by_label = inner_rows(onehot, mixed)
    by_grad = inner_rows(grads, mixed)
    by_label, by_grad = all_reduce(
        jnp.stack([by_label, by_grad]).reshape(2, 64, 8, chans)
    ).reshape(2, count, chans)
    sums = matmul(by_label, value_weight)
    normed, inverse = normalize(sums)
    new_centers = centers + center_gain * normed
    back = matmul(new_centers, key_weight.T) * scale
    logits = matmul(mixed, back.T)
    grad_centers = matmul(by_grad, key_weight) * scale
    grad_key = inner_rows(by_grad, new_centers) * scale
    dnorm = grad_centers * center_gain
    dsums = inverse * (
        dnorm
        - jnp.mean(dnorm, axis=1, keepdims=True)
        - normed * jnp.mean(dnorm * normed, axis=1, keepdims=True)
    )
    grad_value = inner_rows(by_label, dsums)
    dmixed = (matmul(onehot, matmul(dsums, value_weight.T)) + matmul(grads, back)).reshape(
        rows, cols, chans
    )
    rim = padded_2(dmixed, (("row", 0), ("col", 1)), 1)
    grad_features = dmixed
    for a in range(3):
        for b in range(3):
            grad_features = (
                grad_features + depth_kernel[a, b] * rim[2 - a : 2 - a + rows, 2 - b : 2 - b + cols]
            )
    return (
        new_centers,
        logits.reshape(rows, cols, count),
        grad_features,
        grad_centers,
        grad_value,
        grad_key,
    )


def solution(mesh):
    return jax.shard_map(
        shards,
        mesh=mesh,
        in_specs=(
            P("row", "col", None),
            P(),
            P(),
            P(),
            P(),
            P(),
            P("row", "col"),
            P("row", "col", None),
        ),
        out_specs=(P(), P("row", "col", None), P("row", "col", None), P(), P(), P()),
        check_vma=False,
    )
```

```python
import jax
import jax.numpy as jnp
from jax import lax
from jax.experimental import pallas as pl
from jax.experimental.pallas import tpu as pltpu
from jax.sharding import PartitionSpec as P

MESH = pl.DeviceIdType.MESH
HIGH = lax.Precision.HIGH
ROWS, COLS, CHANS, COUNT = 24, 96, 256, 512
GRID_ROWS, GRID_COLS = 16, 8
CELLS = ROWS * COLS
STRIP = 48
NORTH, SOUTH, WEST, EAST = CELLS, CELLS + COLS, CELLS + 2 * COLS, CELLS + 2 * COLS + STRIP
FULL = CELLS + 2 * COLS + 2 * STRIP
SCALE = 1.0 / 16.0
SELF = 42
TILE = (64, 8, 256)
SIDES = ((-1, 0), (1, 0), (0, -1), (0, 1), (-1, -1), (-1, 1), (1, -1), (1, 1))
OPPOSITE = (1, 0, 3, 2, 7, 6, 5, 4)
WHOLE = pl.BlockSpec(memory_space=pltpu.VMEM)
OUTSIDE = pl.BlockSpec(memory_space=pltpu.HBM)


def place():
    r, c = lax.axis_index("row"), lax.axis_index("col")
    return r // 4, lax.rem(r, 4), c // 2, lax.rem(c, 2)


def at(x, y, z, k):
    return (lax.rem(x, 4) * 4 + lax.rem(y, 4), lax.rem(z, 4) * 2 + k)


def chip_at(t):
    x, y, z, k = place()
    x, y, z = x + t // 16 + 2, y + lax.rem(t // 4, 4) + 2, z + lax.rem(t, 4) + 2
    x, y, z = lax.rem(x, 4), lax.rem(y, 4), lax.rem(z, 4)
    return (x * 4 + y, z * 2 + k), x * 16 + y * 4 + z


def signal(sem, device):
    pl.semaphore_signal(sem, inc=1, device_id=device, device_id_type=MESH)


def remote(src, dst, send, recv, device):
    return pltpu.make_async_remote_copy(
        src_ref=src, dst_ref=dst, send_sem=send, recv_sem=recv, device_id=device, device_id_type=MESH
    )


def others(step):
    lax.fori_loop(0, SELF, lambda t, _: step(t, t), None)
    lax.fori_loop(SELF + 1, 64, lambda t, _: step(t, t - 1), None)


def halves(value):
    high = value.astype(jnp.bfloat16)
    return high, (value - high.astype(jnp.float32)).astype(jnp.bfloat16)


def product(left, right, dims=((1,), (0,))):
    return lax.dot_general(left, right, (dims, ((), ())), preferred_element_type=jnp.float32)


def precise(left, right, dims=((1,), (0,))):
    return lax.dot_general(
        left, right, (dims, ((), ())), preferred_element_type=jnp.float32, precision=HIGH
    )


def later(value, edge=None):
    moved = pltpu.roll(value, 1, 0)
    first = lax.broadcasted_iota(jnp.int32, value.shape, 0) == 0
    return jnp.where(first, 0.0 if edge is None else edge, moved)


def earlier(value, edge=None):
    moved = pltpu.roll(value, value.shape[0] - 1, 0)
    last = lax.broadcasted_iota(jnp.int32, value.shape, 0) == value.shape[0] - 1
    return jnp.where(last, 0.0 if edge is None else edge, moved)


def onehot(column, rows):
    clusters = lax.broadcasted_iota(jnp.int32, (rows, COUNT), 1).astype(jnp.float32)
    return jnp.where(column == clusters, 1.0, 0.0).astype(jnp.bfloat16)


def strip_sum(strip, taps):
    return (
        taps[0] * strip[7 : 7 + ROWS, :]
        + taps[1] * strip[8 : 8 + ROWS, :]
        + taps[2] * strip[9 : 9 + ROWS, :]
    )


def halo_copies(own, rows, strips, ends, corners, send, recv, first):
    targets = (
        (own.at[first], rows.at[1]),
        (own.at[first + ROWS - 1], rows.at[0]),
        (ends.at[0], strips.at[1, pl.ds(8, ROWS)]),
        (ends.at[1], strips.at[0, pl.ds(8, ROWS)]),
        (corners.at[0], strips.at[1, pl.ds(32, 8)]),
        (corners.at[1], strips.at[0, pl.ds(32, 8)]),
        (corners.at[2], strips.at[1, pl.ds(0, 8)]),
        (corners.at[3], strips.at[0, pl.ds(0, 8)]),
    )
    return [
        remote(src, dst, send.at[i], recv.at[i], beside(*SIDES[i]))
        for i, (src, dst) in enumerate(targets)
    ]


def beside(dr, dc):
    r, c = lax.axis_index("row"), lax.axis_index("col")
    return (lax.rem(r + dr + GRID_ROWS, GRID_ROWS), lax.rem(c + dc + GRID_COLS, GRID_COLS))


def pack(own, ends, corners, first):
    for i in range(ROWS):
        ends[0, i : i + 1, :] = own[first + i, 0:1, :]
        ends[1, i : i + 1, :] = own[first + i, COLS - 1 : COLS, :]
    for n, (i, j) in enumerate(((0, 0), (0, COLS - 1), (ROWS - 1, 0), (ROWS - 1, COLS - 1))):
        corners[n] = jnp.broadcast_to(own[first + i, j : j + 1, :], corners.shape[1:])


def clear_outside(rows, strips):
    r, c = lax.axis_index("row"), lax.axis_index("col")

    @pl.when(r == 0)
    def _():
        rows[0] = jnp.zeros_like(rows[0])
        for side in range(2):
            strips[side, 0:8, :] = jnp.zeros_like(strips[side, 0:8, :])

    @pl.when(r == GRID_ROWS - 1)
    def _():
        rows[1] = jnp.zeros_like(rows[1])
        for side in range(2):
            strips[side, 32:40, :] = jnp.zeros_like(strips[side, 32:40, :])

    for side, edge in ((0, 0), (1, GRID_COLS - 1)):

        @pl.when(c == edge)
        def _():
            strips[side] = jnp.zeros_like(strips[side])


def reduce_kernel(
    features,
    cotangent,
    labels,
    taps_in,
    sums,
    mixed_pair,
    grads_high,
    grads_low,
    ones,
    fx,
    gx,
    lab,
    taps,
    fn,
    gn,
    fs,
    gs,
    f_ends,
    g_ends,
    f_corners,
    g_corners,
    lab_near,
    lab_square,
    mixed,
    mixed_t,
    rim_t,
    rim_ones,
    rim_high,
    rim_low,
    totals,
    parts,
    partner_part,
    chip_sum,
    landing,
    load,
    met,
    sems,
    f_send,
    f_recv,
    g_send,
    g_recv,
    l_send,
    l_recv,
):
    r, c = lax.axis_index("row"), lax.axis_index("col")
    x, y, z, k = place()
    me = x * 16 + y * 4 + z
    lines = (
        [at(x + d, y, z, k) for d in (1, 2, 3)],
        [at(x, y + d, z, k) for d in (1, 2, 3)],
        [at(x, y, z + d, k) for d in (1, 2, 3)],
    )
    partner = at(x, y, z, 1 - k)
    load_labels = pltpu.make_async_copy(labels, lab, load.at[0])
    load_taps = pltpu.make_async_copy(taps_in, taps, load.at[1])
    load_labels.start()
    load_taps.start()
    load_f = [
        pltpu.make_async_copy(
            features.at[pl.ds(8 * n, 8)], fx.at[pl.ds(1 + 8 * n, 8)], load.at[2 + n]
        )
        for n in range(3)
    ]
    load_g = [
        pltpu.make_async_copy(cotangent.at[pl.ds(8 * n, 8)], gx.at[pl.ds(8 * n, 8)], load.at[5 + n])
        for n in range(3)
    ]
    for copy in (*load_f, *load_g):
        copy.start()
    barrier = pltpu.get_barrier_semaphore()
    for device in [*lines[0], *lines[1], *lines[2], partner, *(beside(*side) for side in SIDES)]:
        signal(barrier, device)

    fx[0] = jnp.zeros_like(fx[0])
    fx[1 + ROWS] = jnp.zeros_like(fx[0])
    load_labels.wait()
    load_taps.wait()
    lab_square[0:ROWS, 0:COLS] = lab[...].astype(jnp.float32)
    by_column = lab_square[...].T
    for i in range(ROWS):
        ones[COLS * i : COLS * (i + 1), :] = onehot(by_column[0:COLS, i : i + 1], COLS)
    for copy in load_f:
        copy.wait()
    pack(fx, f_ends, f_corners, 1)
    for copy in load_g:
        copy.wait()
    pack(gx, g_ends, g_corners, 0)
    pl.semaphore_wait(barrier, 10 + len(SIDES))
    f_copies = halo_copies(fx, fn, fs, f_ends, f_corners, f_send, f_recv, 1)
    g_copies = halo_copies(gx, gn, gs, g_ends, g_corners, g_send, g_recv, 0)
    l_copies = [
        remote(lab, lab_near.at[OPPOSITE[i]], l_send.at[i], l_recv.at[i], beside(*side))
        for i, side in enumerate(SIDES)
    ]
    for copy in f_copies:
        copy.start()
    for device in lines[0]:
        signal(met.at[0], device)
    for copy in (*g_copies, *l_copies):
        copy.start()

    tap = [taps[n // 3, n % 3 : n % 3 + 1] for n in range(9)]

    def mix(i, _):
        above, here, below = fx[i], fx[i + 1], fx[i + 2]
        t = [
            tap[b] * above + tap[3 + b] * here + tap[6 + b] * below for b in range(3)
        ]
        mixed[i] = here + t[1] + later(t[0]) + earlier(t[2])
        cell = pl.ds(pl.multiple_of(i * COLS, COLS), COLS)
        grads_high[cell, :], grads_low[cell, :] = halves(gx[i])

    lax.fori_loop(0, ROWS, mix, None)
    for n in range(9):
        block = mixed[...].reshape(CELLS, CHANS)[256 * n : 256 * (n + 1)].T
        mixed_t[0:256, 256 * n : 256 * (n + 1)], mixed_t[256:512, 256 * n : 256 * (n + 1)] = halves(
            block
        )
    pl.semaphore_wait(met.at[0], 3)
    for device in lines[1]:
        signal(met.at[1], device)
    by_label = product(mixed_t[...], ones[0:CELLS, :])
    totals[0] = by_label[0:256] + by_label[256:512]
    by_grad = product(mixed_t[...], grads_high[0:CELLS, :])
    totals[1] = (
        by_grad[0:256] + by_grad[256:512] + product(mixed_t[0:256, :], grads_low[0:CELLS, :])
    )

    rim_ones[...] = jnp.zeros_like(rim_ones)
    rim_high[...] = jnp.zeros_like(rim_high)
    rim_low[...] = jnp.zeros_like(rim_low)
    for rim, own in ((rim_ones, ones), (rim_high, grads_high), (rim_low, grads_low)):
        rim[0:COLS, :] = own[0:COLS, :]
        rim[COLS : 2 * COLS, :] = own[CELLS - COLS : CELLS, :]
    fill = jnp.zeros((8, COUNT), jnp.float32)
    for side, column in ((0, 0), (1, COLS - 1)):
        cell = slice(192 + 32 * side, 224 + 32 * side)
        rim_high[cell, :], rim_low[cell, :] = halves(
            jnp.concatenate([g_ends[side], fill], axis=0)
        )
        rim_ones[cell, :] = onehot(lab_square[0:32, column : column + 1], 32)

    for copy in f_copies:
        copy.wait_recv()
    clear_outside(fn, fs)
    north = tap[1] * fn[0] + later(tap[0] * fn[0]) + earlier(tap[2] * fn[0])
    south = tap[7] * fn[1] + later(tap[6] * fn[1]) + earlier(tap[8] * fn[1])
    west = strip_sum(fs.at[0], [tap[3 * a] for a in range(3)])
    east = strip_sum(fs.at[1], [tap[3 * a + 2] for a in range(3)])
    gap = jnp.zeros((8, CHANS), jnp.float32)
    rim = jnp.concatenate([north, south, west, gap, east, gap], axis=0)
    rim_t[0:256, :], rim_t[256:512, :] = halves(rim.T)
    by_label = product(rim_t[...], rim_ones[...])
    parts[0] = (totals[0] + by_label[0:256] + by_label[256:512]).T.reshape(TILE)
    by_grad = product(rim_t[...], rim_high[...])
    by_grad = by_grad[0:256] + by_grad[256:512] + product(rim_t[0:256, :], rim_low[...])
    parts[1] = (totals[1] + by_grad).T.reshape(TILE)

    pair = remote(parts.at[1 - k], partner_part, sems.at[0], sems.at[1], partner)
    pair.start()
    pl.semaphore_wait(met.at[1], 3)
    pair.wait()
    chip_sum[...] = parts[k] + partner_part[...]

    def scatter(t, slot):
        device, chip = chip_at(t)
        remote(chip_sum.at[chip], landing.at[slot], sems.at[2], sems.at[3], device).start()

    others(scatter)

    mixed[0] = mixed[0] + north
    mixed[ROWS - 1] = mixed[ROWS - 1] + south
    for i in range(ROWS):
        mixed[i, 0:1, :] = mixed[i, 0:1, :] + west[i : i + 1]
        mixed[i, COLS - 1 : COLS, :] = mixed[i, COLS - 1 : COLS, :] + east[i : i + 1]

    def settle(i, _):
        cell = pl.ds(pl.multiple_of(i * COLS, COLS), COLS)
        mixed_pair[cell, 0:256], mixed_pair[cell, 256:512] = halves(mixed[i])

    lax.fori_loop(0, ROWS, settle, None)

    pltpu.make_async_copy(landing, landing, sems.at[3]).wait()
    sums[k, me] = chip_sum[me] + jnp.sum(landing[...], axis=0)

    def gather(t, slot):
        device, _ = chip_at(t)
        remote(sums.at[k, me], sums.at[k, me], sems.at[4], sems.at[5], device).start()

    others(gather)

    for copy in (*g_copies, *l_copies):
        copy.wait_recv()
    clear_outside(gn, gs)
    for side in range(2):
        for start, value in ((NORTH + side * COLS, gn[side]), (WEST + side * STRIP, gs[side])):
            cell = slice(start, start + value.shape[0])
            grads_high[cell, :], grads_low[cell, :] = halves(value)
    near = [lab_near[i].astype(jnp.float32) for i in range(8)]
    lab_square[0:1, 0:COLS] = jnp.where(r > 0, near[0][ROWS - 1 : ROWS], -1.0)
    lab_square[1:2, 0:COLS] = jnp.where(r < GRID_ROWS - 1, near[1][0:1], -1.0)
    by_column = lab_square[...].T
    ones[NORTH : NORTH + COLS, :] = onehot(by_column[0:COLS, 0:1], COLS)
    ones[SOUTH : SOUTH + COLS, :] = onehot(by_column[0:COLS, 1:2], COLS)
    for side, column, inside in ((0, COLS - 1, c > 0), (1, 0, c < GRID_COLS - 1)):
        place_of = slice(column, column + 1)
        upper, beside_us, lower = near[4 + side], near[2 + side], near[6 + side]
        strip = jnp.concatenate(
            [
                jnp.where(
                    inside & (r > 0),
                    jnp.broadcast_to(upper[ROWS - 1 : ROWS, place_of], (8, 128)),
                    -1.0,
                ),
                jnp.where(inside, jnp.broadcast_to(beside_us[:, place_of], (ROWS, 128)), -1.0),
                jnp.where(
                    inside & (r < GRID_ROWS - 1),
                    jnp.broadcast_to(lower[0:1, place_of], (8, 128)),
                    -1.0,
                ),
                jnp.full((8, 128), -1.0, jnp.float32),
            ],
            axis=0,
        )
        cell = slice(WEST + side * STRIP, WEST + (side + 1) * STRIP)
        ones[cell, :] = onehot(strip[:, 0:1], STRIP)

    pltpu.make_async_copy(landing, landing, sems.at[5]).wait()
    back = remote(sums.at[k], sums.at[k], sems.at[6], sems.at[7], partner)
    back.start()
    pltpu.make_async_copy(landing, landing, sems.at[2]).wait()
    pltpu.make_async_copy(landing, landing, sems.at[4]).wait()
    for copy in (*f_copies, *g_copies, *l_copies):
        copy.wait_send()
    back.wait()


def apply_kernel(
    sums,
    mixed_pair,
    grads_high,
    grads_low,
    ones,
    value_weight,
    key_weight,
    centers,
    gain,
    taps,
    new_centers,
    logits,
    grad_features,
    grad_centers,
    grad_value,
    grad_key,
    new_out,
    logits_out,
    features_out,
    centers_out,
    value_out,
    key_out,
    forth,
    back_pair,
    dm,
    ds,
    small,
    wide,
    grid,
):
    by_label, by_grad = sums[0].reshape(COUNT, CHANS), sums[1].reshape(COUNT, CHANS)
    totals = precise(by_label, value_weight[...])
    centred = totals - jnp.mean(totals, axis=1, keepdims=True)
    inverse = lax.rsqrt(jnp.mean(centred * centred, axis=1, keepdims=True) + 1e-05)
    normed = centred * inverse
    new_out[...] = centers[...] + gain[...] * normed
    copies = [pltpu.make_async_copy(new_out, new_centers, small.at[0])]
    copies[-1].start()
    back = precise(new_out[...], key_weight[...], ((1,), (1,))) * SCALE
    back_high, back_low = halves(back)
    forth_high, forth_low = halves(back.T)
    forth[0:256, :] = forth_high
    forth[256:512, :] = forth_high
    forth[512:768, :] = forth_low
    for n in range(3):
        cell = slice(768 * n, 768 * (n + 1))
        out = product(mixed_pair[cell, :], forth[0:512, :]) + product(
            mixed_pair[cell, 0:256], forth[512:768, :]
        )
        logits_out[8 * n : 8 * (n + 1)] = out.reshape(8, COLS, COUNT)
        copies.append(
            pltpu.make_async_copy(
                logits_out.at[pl.ds(8 * n, 8)], logits.at[pl.ds(8 * n, 8)], wide.at[n]
            )
        )
        copies[-1].start()

    centers_out[...] = precise(by_grad, key_weight[...]) * SCALE
    copies.append(pltpu.make_async_copy(centers_out, grad_centers, small.at[1]))
    copies[-1].start()
    dnorm = centers_out[...] * gain[...]
    dsums = inverse * (
        dnorm
        - jnp.mean(dnorm, axis=1, keepdims=True)
        - normed * jnp.mean(dnorm * normed, axis=1, keepdims=True)
    )
    spread = precise(dsums, value_weight[...], ((1,), (1,)))
    spread_high, spread_low = halves(spread)
    back_pair[0:512] = spread_high
    back_pair[512:1024] = spread_low
    back_pair[1024:1536] = back_high
    back_pair[1536:2048] = back_low

    def dmixed(start, size):
        cell = slice(start, start + size)
        return (
            product(ones[cell, :], back_pair[0:512, :])
            + product(ones[cell, :], back_pair[512:1024, :])
            + product(grads_high[cell, :], back_pair[1024:1536, :])
            + product(grads_low[cell, :], back_pair[1024:1536, :])
            + product(grads_high[cell, :], back_pair[1536:2048, :])
        )

    rim = dmixed(NORTH, FULL - CELLS)
    dm[0] = rim[0:COLS]
    dm[1 + ROWS] = rim[COLS : 2 * COLS]
    ds[0] = rim[2 * COLS : 2 * COLS + STRIP]
    ds[1] = rim[2 * COLS + STRIP :]
    for n in range(3):
        dm[1 + 8 * n : 9 + 8 * n] = dmixed(768 * n, 768).reshape(8, COLS, CHANS)
    value_out[...] = precise(by_label, dsums, ((0,), (0,)))
    key_out[...] = precise(by_grad, new_out[...], ((0,), (0,))) * SCALE
    copies.append(pltpu.make_async_copy(value_out, grad_value, small.at[2]))
    copies[-1].start()
    copies.append(pltpu.make_async_copy(key_out, grad_key, small.at[3]))
    copies[-1].start()

    tap = [taps[2 - n // 3, 2 - n % 3 : 3 - n % 3] for n in range(9)]
    ds[0, 8 : 8 + ROWS, :], ds[1, 8 : 8 + ROWS, :] = (
        strip_sum(ds.at[0], [tap[3 * a] for a in range(3)]),
        strip_sum(ds.at[1], [tap[3 * a + 2] for a in range(3)]),
    )

    def unmix(i, _):
        above, here, below = dm[i], dm[i + 1], dm[i + 2]
        t = [tap[b] * above + tap[3 + b] * here + tap[6 + b] * below for b in range(3)]
        west, east = ds[0, pl.ds(8 + i, 1), :], ds[1, pl.ds(8 + i, 1), :]
        features_out[i] = here + t[1] + later(t[0], west) + earlier(t[2], east)

    for n in range(3):
        lax.fori_loop(8 * n, 8 * (n + 1), unmix, None)
        copies.append(
            pltpu.make_async_copy(
                features_out.at[pl.ds(8 * n, 8)], grad_features.at[pl.ds(8 * n, 8)], grid.at[n]
            )
        )
        copies[-1].start()
    for copy in copies:
        copy.wait()


def shards(
    features, depth_kernel, value_weight, key_weight, centers, center_gain, labels, cotangent
):
    f32, b16, vm, dma = jnp.float32, jnp.bfloat16, pltpu.VMEM, pltpu.SemaphoreType.DMA
    features, cotangent, labels, taps = (
        pltpu.with_memory_space_constraint(value, pltpu.HBM)
        for value in (features, cotangent, labels, depth_kernel)
    )
    held = pl.pallas_call(
        reduce_kernel,
        out_shape=(
            vm((2, *TILE), f32),
            vm((CELLS, 2 * CHANS), b16),
            vm((FULL, COUNT), b16),
            vm((FULL, COUNT), b16),
            vm((FULL, COUNT), b16),
        ),
        in_specs=[OUTSIDE] * 4,
        out_specs=[WHOLE] * 5,
        scratch_shapes=[
            vm((2 + ROWS, COLS, CHANS), f32),
            vm((ROWS, COLS, COUNT), f32),
            vm((ROWS, COLS), jnp.int32),
            vm((3, 3, CHANS), f32),
            vm((2, COLS, CHANS), f32),
            vm((2, COLS, COUNT), f32),
            vm((2, STRIP, CHANS), f32),
            vm((2, STRIP, COUNT), f32),
            vm((2, ROWS, CHANS), f32),
            vm((2, ROWS, COUNT), f32),
            vm((4, 8, CHANS), f32),
            vm((4, 8, COUNT), f32),
            vm((8, ROWS, COLS), jnp.int32),
            vm((128, 128), f32),
            vm((ROWS, COLS, CHANS), f32),
            vm((2 * CHANS, CELLS), b16),
            vm((2 * CHANS, 256), b16),
            vm((256, COUNT), b16),
            vm((256, COUNT), b16),
            vm((256, COUNT), b16),
            vm((2, CHANS, COUNT), f32),
            vm((2, *TILE), f32),
            vm(TILE, f32),
            vm(TILE, f32),
            vm((63, 8, 256), f32),
            dma((8,)),
            pltpu.SemaphoreType.REGULAR((2,)),
            dma((8,)),
            *[dma((8,))] * 6,
        ],
        compiler_params=pltpu.CompilerParams(
            collective_id=0, has_side_effects=True, vmem_limit_bytes=30 * 2**20
        ),
    )(features, cotangent, labels, taps)
    return pl.pallas_call(
        apply_kernel,
        out_shape=(
            jax.ShapeDtypeStruct((COUNT, CHANS), f32),
            jax.ShapeDtypeStruct((ROWS, COLS, COUNT), f32),
            jax.ShapeDtypeStruct((ROWS, COLS, CHANS), f32),
            jax.ShapeDtypeStruct((COUNT, CHANS), f32),
            jax.ShapeDtypeStruct((CHANS, CHANS), f32),
            jax.ShapeDtypeStruct((CHANS, CHANS), f32),
        ),
        in_specs=[WHOLE] * 10,
        out_specs=[OUTSIDE] * 6,
        scratch_shapes=[
            vm((COUNT, CHANS), f32),
            vm((ROWS, COLS, COUNT), f32),
            vm((ROWS, COLS, CHANS), f32),
            vm((COUNT, CHANS), f32),
            vm((CHANS, CHANS), f32),
            vm((CHANS, CHANS), f32),
            vm((768, COUNT), b16),
            vm((2048, CHANS), b16),
            vm((2 + ROWS, COLS, CHANS), f32),
            vm((2, STRIP, CHANS), f32),
            dma((4,)),
            dma((3,)),
            dma((3,)),
        ],
        compiler_params=pltpu.CompilerParams(vmem_limit_bytes=30 * 2**20),
    )(*held, value_weight, key_weight, centers, center_gain.reshape(1, CHANS), depth_kernel)


def solution(mesh):
    return jax.shard_map(
        shards,
        mesh=mesh,
        in_specs=(
            P("row", "col", None),
            P(),
            P(),
            P(),
            P(),
            P(),
            P("row", "col"),
            P("row", "col", None),
        ),
        out_specs=(P(), P("row", "col", None), P("row", "col", None), P(), P(), P()),
        check_vma=False,
    )
```

```python
import jax
import jax.numpy as jnp
from jax import lax
from jax.experimental import pallas as pl
from jax.experimental.pallas import tpu as pltpu
from jax.sharding import PartitionSpec as P

MESH = pl.DeviceIdType.MESH
HIGH = lax.Precision.HIGH
ROWS, COLS, CHANS, COUNT = 24, 96, 256, 512
GRID_ROWS, GRID_COLS = 16, 8
CELLS = ROWS * COLS
STRIP = 48
NORTH, SOUTH, WEST, EAST = CELLS, CELLS + COLS, CELLS + 2 * COLS, CELLS + 2 * COLS + STRIP
FULL = CELLS + 2 * COLS + 2 * STRIP
SCALE = 1.0 / 16.0
ONES, UPPER, LOWER = slice(0, 512), slice(512, 1024), slice(1024, 1536)
ORDER = (
    42, 38, 46, 41, 43, 58, 26, 37, 59, 25, 39, 34, 22, 62, 54, 47, 57, 40, 30, 45, 27,
    10, 9, 55, 29, 31, 14, 61, 50, 53, 18, 21, 35, 24, 56, 44, 11, 33, 23, 6, 36, 63,
    52, 49, 5, 17, 8, 32, 7, 2, 28, 15, 51, 60, 13, 19, 20, 1, 48, 16, 12, 4, 3,
)
TILE = (64, 8, 256)
SIDES = ((-1, 0), (1, 0), (0, -1), (0, 1), (-1, -1), (-1, 1), (1, -1), (1, 1))
OPPOSITE = (1, 0, 3, 2, 7, 6, 5, 4)
WHOLE = pl.BlockSpec(memory_space=pltpu.VMEM)
OUTSIDE = pl.BlockSpec(memory_space=pltpu.HBM)


def place():
    r, c = lax.axis_index("row"), lax.axis_index("col")
    return r // 4, lax.rem(r, 4), c // 2, lax.rem(c, 2)


def at(x, y, z, k):
    return (lax.rem(x, 4) * 4 + lax.rem(y, 4), lax.rem(z, 4) * 2 + k)


def chip_at(code):
    x, y, z, k = place()
    x, y, z = x + code // 16, y + code // 4 % 4, z + code % 4
    x, y, z = lax.rem(x, 4), lax.rem(y, 4), lax.rem(z, 4)
    return (x * 4 + y, z * 2 + k), x * 16 + y * 4 + z


def opposite(code):
    x, y, z = code // 16, code // 4 % 4, code % 4
    return -x % 4 * 16 + -y % 4 * 4 + -z % 4


def signal(sem, device):
    pl.semaphore_signal(sem, inc=1, device_id=device, device_id_type=MESH)


def remote(src, dst, send, recv, device):
    return pltpu.make_async_remote_copy(
        src_ref=src, dst_ref=dst, send_sem=send, recv_sem=recv, device_id=device, device_id_type=MESH
    )


def halves(value):
    high = value.astype(jnp.bfloat16)
    return high, (value - high.astype(jnp.float32)).astype(jnp.bfloat16)


def product(left, right, dims=((1,), (0,))):
    return lax.dot_general(left, right, (dims, ((), ())), preferred_element_type=jnp.float32)


def precise(left, right, dims=((1,), (0,))):
    return lax.dot_general(
        left, right, (dims, ((), ())), preferred_element_type=jnp.float32, precision=HIGH
    )


def later(value, edge=None):
    moved = pltpu.roll(value, 1, 0)
    first = lax.broadcasted_iota(jnp.int32, value.shape, 0) == 0
    return jnp.where(first, 0.0 if edge is None else edge, moved)


def earlier(value, edge=None):
    moved = pltpu.roll(value, value.shape[0] - 1, 0)
    last = lax.broadcasted_iota(jnp.int32, value.shape, 0) == value.shape[0] - 1
    return jnp.where(last, 0.0 if edge is None else edge, moved)


def onehot(column, rows):
    clusters = lax.broadcasted_iota(jnp.int32, (rows, COUNT), 1).astype(jnp.float32)
    return jnp.where(column == clusters, 1.0, 0.0).astype(jnp.bfloat16)


def strip_sum(strip, taps):
    return (
        taps[0] * strip[7 : 7 + ROWS, :]
        + taps[1] * strip[8 : 8 + ROWS, :]
        + taps[2] * strip[9 : 9 + ROWS, :]
    )


def halo_copies(own, rows, strips, ends, corners, send, recv, first):
    targets = (
        (own.at[first], rows.at[1]),
        (own.at[first + ROWS - 1], rows.at[0]),
        (ends.at[0], strips.at[1, pl.ds(8, ROWS)]),
        (ends.at[1], strips.at[0, pl.ds(8, ROWS)]),
        (corners.at[0], strips.at[1, pl.ds(32, 8)]),
        (corners.at[1], strips.at[0, pl.ds(32, 8)]),
        (corners.at[2], strips.at[1, pl.ds(0, 8)]),
        (corners.at[3], strips.at[0, pl.ds(0, 8)]),
    )
    return [
        remote(src, dst, send.at[i], recv.at[i], beside(*SIDES[i]))
        for i, (src, dst) in enumerate(targets)
    ]


def beside(dr, dc):
    r, c = lax.axis_index("row"), lax.axis_index("col")
    return (lax.rem(r + dr + GRID_ROWS, GRID_ROWS), lax.rem(c + dc + GRID_COLS, GRID_COLS))


def pack(own, ends, corners, first):
    for i in range(ROWS):
        ends[0, i : i + 1, :] = own[first + i, 0:1, :]
        ends[1, i : i + 1, :] = own[first + i, COLS - 1 : COLS, :]
    for n, (i, j) in enumerate(((0, 0), (0, COLS - 1), (ROWS - 1, 0), (ROWS - 1, COLS - 1))):
        corners[n] = jnp.broadcast_to(own[first + i, j : j + 1, :], corners.shape[1:])


def clear_outside(rows, strips):
    r, c = lax.axis_index("row"), lax.axis_index("col")

    @pl.when(r == 0)
    def _():
        rows[0] = jnp.zeros_like(rows[0])
        for side in range(2):
            strips[side, 0:8, :] = jnp.zeros_like(strips[side, 0:8, :])

    @pl.when(r == GRID_ROWS - 1)
    def _():
        rows[1] = jnp.zeros_like(rows[1])
        for side in range(2):
            strips[side, 32:40, :] = jnp.zeros_like(strips[side, 32:40, :])

    for side, edge in ((0, 0), (1, GRID_COLS - 1)):

        @pl.when(c == edge)
        def _():
            strips[side] = jnp.zeros_like(strips[side])


def reduce_kernel(
    features,
    cotangent,
    labels,
    taps_in,
    sums,
    mixed_pair,
    acts,
    fx,
    gx,
    lab,
    taps,
    fn,
    gn,
    fs,
    gs,
    f_ends,
    g_ends,
    f_corners,
    g_corners,
    lab_near,
    lab_square,
    mixed,
    mixed_t,
    rim_t,
    rim_acts,
    totals,
    parts,
    partner_part,
    chip_sum,
    landing,
    load,
    met,
    sems,
    got,
    f_send,
    f_recv,
    g_send,
    g_recv,
    l_send,
    l_recv,
):
    r, c = lax.axis_index("row"), lax.axis_index("col")
    x, y, z, k = place()
    me = x * 16 + y * 4 + z
    lines = (
        [at(x + d, y, z, k) for d in (1, 2, 3)],
        [at(x, y + d, z, k) for d in (1, 2, 3)],
        [at(x, y, z + d, k) for d in (1, 2, 3)],
    )
    partner = at(x, y, z, 1 - k)
    load_labels = pltpu.make_async_copy(labels, lab, load.at[0])
    load_taps = pltpu.make_async_copy(taps_in, taps, load.at[1])
    load_labels.start()
    load_taps.start()
    load_f = [
        pltpu.make_async_copy(
            features.at[pl.ds(8 * n, 8)], fx.at[pl.ds(1 + 8 * n, 8)], load.at[2 + n]
        )
        for n in range(3)
    ]
    load_g = [
        pltpu.make_async_copy(cotangent.at[pl.ds(8 * n, 8)], gx.at[pl.ds(8 * n, 8)], load.at[5 + n])
        for n in range(3)
    ]
    for copy in (*load_f, *load_g):
        copy.start()
    barrier = pltpu.get_barrier_semaphore()
    for device in [*lines[0], *lines[1], *lines[2], partner, *(beside(*side) for side in SIDES)]:
        signal(barrier, device)

    fx[0] = jnp.zeros_like(fx[0])
    fx[1 + ROWS] = jnp.zeros_like(fx[0])
    load_labels.wait()
    load_taps.wait()
    lab_square[0:ROWS, 0:COLS] = lab[...].astype(jnp.float32)
    by_column = lab_square[...].T
    for i in range(ROWS):
        acts[COLS * i : COLS * (i + 1), ONES] = onehot(by_column[0:COLS, i : i + 1], COLS)
    for copy in load_f:
        copy.wait()
    pack(fx, f_ends, f_corners, 1)
    f_copies = halo_copies(fx, fn, fs, f_ends, f_corners, f_send, f_recv, 1)
    g_copies = halo_copies(gx, gn, gs, g_ends, g_corners, g_send, g_recv, 0)
    l_copies = [
        remote(lab, lab_near.at[OPPOSITE[i]], l_send.at[i], l_recv.at[i], beside(*side))
        for i, side in enumerate(SIDES)
    ]
    tap = [taps[n // 3, n % 3 : n % 3 + 1] for n in range(9)]

    def mix(n):
        for i in range(8 * n, 8 * (n + 1)):
            above, here, below = fx[i], fx[i + 1], fx[i + 2]
            t = [tap[b] * above + tap[3 + b] * here + tap[6 + b] * below for b in range(3)]
            mixed[i] = here + t[1] + later(t[0]) + earlier(t[2])
        block = mixed[8 * n : 8 * (n + 1)].reshape(768, CHANS)
        for m in range(3):
            cell = slice(768 * n + 256 * m, 768 * n + 256 * (m + 1))
            mixed_t[0:256, cell], mixed_t[256:512, cell] = halves(
                block[256 * m : 256 * (m + 1)].T
            )

    def split(n):
        for i in range(8 * n, 8 * (n + 1)):
            cell = slice(COLS * i, COLS * (i + 1))
            acts[cell, UPPER], acts[cell, LOWER] = halves(gx[i])

    def add(which, n, value):
        totals[which] = value if n == 0 else totals[which] + value

    def sum_labels(n):
        cell = slice(768 * n, 768 * (n + 1))
        value = product(mixed_t[:, cell], acts[cell, ONES])
        add(0, n, value[0:256] + value[256:512])

    def sum_grads(n):
        cell = slice(768 * n, 768 * (n + 1))
        value = product(mixed_t[:, cell], acts[cell, UPPER])
        more = product(mixed_t[0:256, cell], acts[cell, LOWER])
        add(1, n, value[0:256] + value[256:512] + more)

    mix(0)
    sum_labels(0)
    mix(1)
    pl.semaphore_wait(barrier, 10 + len(SIDES))
    for copy in f_copies:
        copy.start()
    for device in lines[0]:
        signal(met.at[0], device)
    for copy in l_copies:
        copy.start()
    sum_labels(1)
    mix(2)
    for copy in load_g:
        copy.wait()
    pack(gx, g_ends, g_corners, 0)
    for copy in g_copies:
        copy.start()
    sum_labels(2)
    split(0)
    sum_grads(0)
    split(1)
    sum_grads(1)
    split(2)
    pl.semaphore_wait(met.at[0], 3)
    for device in lines[1]:
        signal(met.at[1], device)
    sum_grads(2)

    rim_acts[...] = jnp.zeros_like(rim_acts)
    rim_acts[0:COLS, :] = acts[0:COLS, :]
    rim_acts[COLS : 2 * COLS, :] = acts[CELLS - COLS : CELLS, :]
    fill = jnp.zeros((8, COUNT), jnp.float32)
    for side, column in ((0, 0), (1, COLS - 1)):
        cell = slice(192 + 32 * side, 224 + 32 * side)
        rim_acts[cell, UPPER], rim_acts[cell, LOWER] = halves(
            jnp.concatenate([g_ends[side], fill], axis=0)
        )
        rim_acts[cell, ONES] = onehot(lab_square[0:32, column : column + 1], 32)

    for copy in f_copies:
        copy.wait_recv()
    clear_outside(fn, fs)
    north = tap[1] * fn[0] + later(tap[0] * fn[0]) + earlier(tap[2] * fn[0])
    south = tap[7] * fn[1] + later(tap[6] * fn[1]) + earlier(tap[8] * fn[1])
    west = strip_sum(fs.at[0], [tap[3 * a] for a in range(3)])
    east = strip_sum(fs.at[1], [tap[3 * a + 2] for a in range(3)])
    gap = jnp.zeros((8, CHANS), jnp.float32)
    rim = jnp.concatenate([north, south, west, gap, east, gap], axis=0)
    rim_t[0:256, :], rim_t[256:512, :] = halves(rim.T)
    by_label = product(rim_t[...], rim_acts[:, ONES])
    parts[0] = (totals[0] + by_label[0:256] + by_label[256:512]).T.reshape(TILE)
    by_grad = product(rim_t[...], rim_acts[:, UPPER])
    by_grad = by_grad[0:256] + by_grad[256:512] + product(rim_t[0:256, :], rim_acts[:, LOWER])
    parts[1] = (totals[1] + by_grad).T.reshape(TILE)

    pair = remote(parts.at[1 - k], partner_part, sems.at[0], sems.at[1], partner)
    pair.start()
    pl.semaphore_wait(met.at[1], 3)
    pair.wait()
    chip_sum[...] = parts[k] + partner_part[...]

    for slot, code in enumerate(ORDER):
        device, chip = chip_at(code)
        remote(chip_sum.at[chip], landing.at[slot], sems.at[2], sems.at[3], device).start()

    mixed[0] = mixed[0] + north
    mixed[ROWS - 1] = mixed[ROWS - 1] + south
    for i in range(ROWS):
        mixed[i, 0:1, :] = mixed[i, 0:1, :] + west[i : i + 1]
        mixed[i, COLS - 1 : COLS, :] = mixed[i, COLS - 1 : COLS, :] + east[i : i + 1]

    def settle(i, _):
        cell = pl.ds(pl.multiple_of(i * COLS, COLS), COLS)
        mixed_pair[cell, 0:256], mixed_pair[cell, 256:512] = halves(mixed[i])

    lax.fori_loop(0, ROWS, settle, None)

    pltpu.make_async_copy(landing, landing, sems.at[3]).wait()
    sums[k, me] = chip_sum[me] + jnp.sum(landing[...], axis=0)

    for slot, code in enumerate(ORDER):
        device, _ = chip_at(code)
        remote(sums.at[k, me], sums.at[k, me], sems.at[4], got.at[slot // 21], device).start()

    for copy in (*g_copies, *l_copies):
        copy.wait_recv()
    clear_outside(gn, gs)
    for side in range(2):
        for start, value in ((NORTH + side * COLS, gn[side]), (WEST + side * STRIP, gs[side])):
            cell = slice(start, start + value.shape[0])
            acts[cell, UPPER], acts[cell, LOWER] = halves(value)
    near = [lab_near[i].astype(jnp.float32) for i in range(8)]
    lab_square[0:1, 0:COLS] = jnp.where(r > 0, near[0][ROWS - 1 : ROWS], -1.0)
    lab_square[1:2, 0:COLS] = jnp.where(r < GRID_ROWS - 1, near[1][0:1], -1.0)
    by_column = lab_square[...].T
    acts[NORTH : NORTH + COLS, ONES] = onehot(by_column[0:COLS, 0:1], COLS)
    acts[SOUTH : SOUTH + COLS, ONES] = onehot(by_column[0:COLS, 1:2], COLS)
    for side, column, inside in ((0, COLS - 1, c > 0), (1, 0, c < GRID_COLS - 1)):
        place_of = slice(column, column + 1)
        upper, beside_us, lower = near[4 + side], near[2 + side], near[6 + side]
        strip = jnp.concatenate(
            [
                jnp.where(
                    inside & (r > 0),
                    jnp.broadcast_to(upper[ROWS - 1 : ROWS, place_of], (8, 128)),
                    -1.0,
                ),
                jnp.where(inside, jnp.broadcast_to(beside_us[:, place_of], (ROWS, 128)), -1.0),
                jnp.where(
                    inside & (r < GRID_ROWS - 1),
                    jnp.broadcast_to(lower[0:1, place_of], (8, 128)),
                    -1.0,
                ),
                jnp.full((8, 128), -1.0, jnp.float32),
            ],
            axis=0,
        )
        cell = slice(WEST + side * STRIP, WEST + (side + 1) * STRIP)
        acts[cell, ONES] = onehot(strip[:, 0:1], STRIP)

    slab = sums.at[k, me]
    remote(slab, slab, sems.at[6], sems.at[7], partner).start()
    for group in range(3):
        block = landing.at[pl.ds(0, 21)]
        pltpu.make_async_copy(block, block, got.at[group]).wait()
        for code in ORDER[21 * group : 21 * (group + 1)]:
            _, chip = chip_at(opposite(code))
            slab = sums.at[k, chip]
            remote(slab, slab, sems.at[6], sems.at[7], partner).start()
    pltpu.make_async_copy(landing, landing, sems.at[2]).wait()
    pltpu.make_async_copy(landing, landing, sems.at[4]).wait()
    for copy in (*f_copies, *g_copies, *l_copies):
        copy.wait_send()
    half = sums.at[k]
    remote(half, half, sems.at[6], sems.at[7], partner).wait()


def apply_kernel(
    sums,
    mixed_pair,
    acts,
    value_weight,
    key_weight,
    centers,
    gain,
    taps,
    new_centers,
    logits,
    grad_features,
    grad_centers,
    grad_value,
    grad_key,
    new_out,
    logits_out,
    features_out,
    centers_out,
    value_out,
    key_out,
    forth,
    back_pair,
    dm,
    ds,
    small,
    wide,
    grid,
):
    by_label, by_grad = sums[0].reshape(COUNT, CHANS), sums[1].reshape(COUNT, CHANS)
    totals = precise(by_label, value_weight[...])
    centers_out[...] = precise(by_grad, key_weight[...]) * SCALE
    centred = totals - jnp.mean(totals, axis=1, keepdims=True)
    inverse = lax.rsqrt(jnp.mean(centred * centred, axis=1, keepdims=True) + 1e-05)
    normed = centred * inverse
    new_out[...] = centers[...] + gain[...] * normed
    back = precise(new_out[...], key_weight[...], ((1,), (1,))) * SCALE
    back_high, back_low = halves(back)
    forth_high, forth_low = halves(back.T)
    forth[0:256, :] = forth_high
    forth[256:512, :] = forth_high
    forth[512:768, :] = forth_low
    dnorm = centers_out[...] * gain[...]
    dsums = inverse * (
        dnorm
        - jnp.mean(dnorm, axis=1, keepdims=True)
        - normed * jnp.mean(dnorm * normed, axis=1, keepdims=True)
    )
    spread = precise(dsums, value_weight[...], ((1,), (1,)))
    spread_high, spread_low = halves(spread)
    back_pair[0:512] = spread_high
    back_pair[512:1024] = back_high
    back_pair[1024:1536] = back_high
    back_pair[1536:2048] = spread_low
    back_pair[2048:2560] = back_low
    copies = []

    def send(out, to, sem):
        copies.append(pltpu.make_async_copy(out, to, sem))
        copies[-1].start()

    def project(n):
        cell = slice(384 * n, 384 * (n + 1))
        out = product(mixed_pair[cell, :], forth[0:512, :]) + product(
            mixed_pair[cell, 0:256], forth[512:768, :]
        )
        logits_out[4 * n : 4 * (n + 1)] = out.reshape(4, COLS, COUNT)

    def dmixed(start, size):
        cell = slice(start, start + size)
        return product(acts[cell, :], back_pair[0:1536, :]) + product(
            acts[cell, 0:1024], back_pair[1536:2560, :]
        )

    def spread_cells(n):
        dm[1 + 4 * n : 5 + 4 * n] = dmixed(384 * n, 384).reshape(4, COLS, CHANS)

    tap = [taps[2 - n // 3, 2 - n % 3 : 3 - n % 3] for n in range(9)]

    def unmix(n):
        for i in range(4 * n, 4 * (n + 1)):
            above, here, below = dm[i], dm[i + 1], dm[i + 2]
            t = [tap[b] * above + tap[3 + b] * here + tap[6 + b] * below for b in range(3)]
            west, east = west_rim[i : i + 1], east_rim[i : i + 1]
            features_out[i] = here + t[1] + later(t[0], west) + earlier(t[2], east)

    for n in range(6):
        project(n)
        if n % 2:
            rows = pl.ds(4 * (n - 1), 8)
            send(logits_out.at[rows], logits.at[rows], wide.at[n // 2])
    send(new_out, new_centers, small.at[0])
    send(centers_out, grad_centers, small.at[1])
    rim = dmixed(NORTH, FULL - CELLS)
    dm[0] = rim[0:COLS]
    dm[1 + ROWS] = rim[COLS : 2 * COLS]
    ds[0] = rim[2 * COLS : 2 * COLS + STRIP]
    ds[1] = rim[2 * COLS + STRIP :]
    west_rim = strip_sum(ds.at[0], [tap[3 * a] for a in range(3)])
    east_rim = strip_sum(ds.at[1], [tap[3 * a + 2] for a in range(3)])
    spread_cells(0)
    spread_cells(1)
    for n in range(6):
        unmix(n)
        if n < 4:
            spread_cells(n + 2)
        if n == 4:
            value_out[...] = precise(by_label, dsums, ((0,), (0,)))
            key_out[...] = precise(by_grad, new_out[...], ((0,), (0,))) * SCALE
            send(value_out, grad_value, small.at[2])
            send(key_out, grad_key, small.at[3])
        if n % 2:
            rows = pl.ds(4 * (n - 1), 8)
            send(features_out.at[rows], grad_features.at[rows], grid.at[n // 2])
    for copy in copies:
        copy.wait()


def shards(
    features, depth_kernel, value_weight, key_weight, centers, center_gain, labels, cotangent
):
    f32, b16, vm, dma = jnp.float32, jnp.bfloat16, pltpu.VMEM, pltpu.SemaphoreType.DMA
    features, cotangent, labels, taps = (
        pltpu.with_memory_space_constraint(value, pltpu.HBM)
        for value in (features, cotangent, labels, depth_kernel)
    )
    held = pl.pallas_call(
        reduce_kernel,
        out_shape=(
            vm((2, *TILE), f32),
            vm((CELLS, 2 * CHANS), b16),
            vm((FULL, 3 * COUNT), b16),
        ),
        in_specs=[OUTSIDE] * 4,
        out_specs=[WHOLE] * 3,
        scratch_shapes=[
            vm((2 + ROWS, COLS, CHANS), f32),
            vm((ROWS, COLS, COUNT), f32),
            vm((ROWS, COLS), jnp.int32),
            vm((3, 3, CHANS), f32),
            vm((2, COLS, CHANS), f32),
            vm((2, COLS, COUNT), f32),
            vm((2, STRIP, CHANS), f32),
            vm((2, STRIP, COUNT), f32),
            vm((2, ROWS, CHANS), f32),
            vm((2, ROWS, COUNT), f32),
            vm((4, 8, CHANS), f32),
            vm((4, 8, COUNT), f32),
            vm((8, ROWS, COLS), jnp.int32),
            vm((128, 128), f32),
            vm((ROWS, COLS, CHANS), f32),
            vm((2 * CHANS, CELLS), b16),
            vm((2 * CHANS, 256), b16),
            vm((256, 3 * COUNT), b16),
            vm((2, CHANS, COUNT), f32),
            vm((2, *TILE), f32),
            vm(TILE, f32),
            vm(TILE, f32),
            vm((63, 8, 256), f32),
            dma((8,)),
            pltpu.SemaphoreType.REGULAR((2,)),
            dma((8,)),
            dma((3,)),
            *[dma((8,))] * 6,
        ],
        compiler_params=pltpu.CompilerParams(
            collective_id=0, has_side_effects=True, vmem_limit_bytes=30 * 2**20
        ),
    )(features, cotangent, labels, taps)
    return pl.pallas_call(
        apply_kernel,
        out_shape=(
            jax.ShapeDtypeStruct((COUNT, CHANS), f32),
            jax.ShapeDtypeStruct((ROWS, COLS, COUNT), f32),
            jax.ShapeDtypeStruct((ROWS, COLS, CHANS), f32),
            jax.ShapeDtypeStruct((COUNT, CHANS), f32),
            jax.ShapeDtypeStruct((CHANS, CHANS), f32),
            jax.ShapeDtypeStruct((CHANS, CHANS), f32),
        ),
        in_specs=[WHOLE] * 8,
        out_specs=[OUTSIDE] * 6,
        scratch_shapes=[
            vm((COUNT, CHANS), f32),
            vm((ROWS, COLS, COUNT), f32),
            vm((ROWS, COLS, CHANS), f32),
            vm((COUNT, CHANS), f32),
            vm((CHANS, CHANS), f32),
            vm((CHANS, CHANS), f32),
            vm((768, COUNT), b16),
            vm((2560, CHANS), b16),
            vm((2 + ROWS, COLS, CHANS), f32),
            vm((2, STRIP, CHANS), f32),
            dma((4,)),
            dma((3,)),
            dma((3,)),
        ],
        compiler_params=pltpu.CompilerParams(vmem_limit_bytes=30 * 2**20),
    )(*held, value_weight, key_weight, centers, center_gain.reshape(1, CHANS), depth_kernel)


def solution(mesh):
    return jax.shard_map(
        shards,
        mesh=mesh,
        in_specs=(
            P("row", "col", None),
            P(),
            P(),
            P(),
            P(),
            P(),
            P("row", "col"),
            P("row", "col", None),
        ),
        out_specs=(P(), P("row", "col", None), P("row", "col", None), P(), P(), P()),
        check_vma=False,
    )
```

```python
import jax
import jax.numpy as jnp
from jax import lax
from jax.experimental import pallas as pl
from jax.experimental.pallas import tpu as pltpu
from jax.sharding import PartitionSpec as P

MESH = pl.DeviceIdType.MESH
HIGH = lax.Precision.HIGH
ROWS, COLS, CHANS, COUNT = 24, 96, 256, 512
GRID_ROWS, GRID_COLS = 16, 8
CELLS = ROWS * COLS
STRIP = 48
NORTH, SOUTH, WEST, EAST = CELLS, CELLS + COLS, CELLS + 2 * COLS, CELLS + 2 * COLS + STRIP
FULL = CELLS + 2 * COLS + 2 * STRIP
SCALE = 1.0 / 16.0
ONES, UPPER, LOWER = slice(0, 512), slice(512, 1024), slice(1024, 1536)
ORDER = (
    42, 38, 46, 41, 43, 58, 26, 37, 59, 25, 39, 34, 22, 62, 54, 47, 57, 40, 30, 45, 27,
    10, 9, 55, 29, 31, 14, 61, 50, 53, 18, 21, 35, 24, 56, 44, 11, 33, 23, 6, 36, 63,
    52, 49, 5, 17, 8, 32, 7, 2, 28, 15, 51, 60, 13, 19, 20, 1, 48, 16, 12, 4, 3,
)
TILE = (64, 8, 256)
SIDES = ((-1, 0), (1, 0), (0, -1), (0, 1), (-1, -1), (-1, 1), (1, -1), (1, 1))
OPPOSITE = (1, 0, 3, 2, 7, 6, 5, 4)
WHOLE = pl.BlockSpec(memory_space=pltpu.VMEM)
OUTSIDE = pl.BlockSpec(memory_space=pltpu.HBM)


def place():
    r, c = lax.axis_index("row"), lax.axis_index("col")
    return r // 4, lax.rem(r, 4), c // 2, lax.rem(c, 2)


def at(x, y, z, k):
    return (lax.rem(x, 4) * 4 + lax.rem(y, 4), lax.rem(z, 4) * 2 + k)


def chip_at(code):
    x, y, z, k = place()
    x, y, z = x + code // 16, y + code // 4 % 4, z + code % 4
    x, y, z = lax.rem(x, 4), lax.rem(y, 4), lax.rem(z, 4)
    return (x * 4 + y, z * 2 + k), x * 16 + y * 4 + z


def opposite(code):
    x, y, z = code // 16, code // 4 % 4, code % 4
    return -x % 4 * 16 + -y % 4 * 4 + -z % 4


def signal(sem, device):
    pl.semaphore_signal(sem, inc=1, device_id=device, device_id_type=MESH)


def remote(src, dst, send, recv, device):
    return pltpu.make_async_remote_copy(
        src_ref=src, dst_ref=dst, send_sem=send, recv_sem=recv, device_id=device, device_id_type=MESH
    )


def halves(value):
    high = value.astype(jnp.bfloat16)
    return high, (value - high.astype(jnp.float32)).astype(jnp.bfloat16)


def product(left, right, dims=((1,), (0,))):
    return lax.dot_general(left, right, (dims, ((), ())), preferred_element_type=jnp.float32)


def precise(left, right, dims=((1,), (0,))):
    return lax.dot_general(
        left, right, (dims, ((), ())), preferred_element_type=jnp.float32, precision=HIGH
    )


def later(value, edge=None):
    moved = pltpu.roll(value, 1, 0)
    first = lax.broadcasted_iota(jnp.int32, value.shape, 0) == 0
    return jnp.where(first, 0.0 if edge is None else edge, moved)


def earlier(value, edge=None):
    moved = pltpu.roll(value, value.shape[0] - 1, 0)
    last = lax.broadcasted_iota(jnp.int32, value.shape, 0) == value.shape[0] - 1
    return jnp.where(last, 0.0 if edge is None else edge, moved)


def onehot(column, rows):
    clusters = lax.broadcasted_iota(jnp.int32, (rows, COUNT), 1).astype(jnp.float32)
    return jnp.where(column == clusters, 1.0, 0.0).astype(jnp.bfloat16)


def strip_sum(strip, taps):
    return (
        taps[0] * strip[7 : 7 + ROWS, :]
        + taps[1] * strip[8 : 8 + ROWS, :]
        + taps[2] * strip[9 : 9 + ROWS, :]
    )


def halo_copies(own, rows, strips, ends, corners, send, recv, first):
    targets = (
        (own.at[first], rows.at[1]),
        (own.at[first + ROWS - 1], rows.at[0]),
        (ends.at[0], strips.at[1, pl.ds(8, ROWS)]),
        (ends.at[1], strips.at[0, pl.ds(8, ROWS)]),
        (corners.at[0], strips.at[1, pl.ds(32, 8)]),
        (corners.at[1], strips.at[0, pl.ds(32, 8)]),
        (corners.at[2], strips.at[1, pl.ds(0, 8)]),
        (corners.at[3], strips.at[0, pl.ds(0, 8)]),
    )
    return [
        remote(src, dst, send.at[i], recv.at[i], beside(*SIDES[i]))
        for i, (src, dst) in enumerate(targets)
    ]


def beside(dr, dc):
    r, c = lax.axis_index("row"), lax.axis_index("col")
    return (lax.rem(r + dr + GRID_ROWS, GRID_ROWS), lax.rem(c + dc + GRID_COLS, GRID_COLS))


def pack(own, ends, corners, first):
    for i in range(ROWS):
        ends[0, i : i + 1, :] = own[first + i, 0:1, :]
        ends[1, i : i + 1, :] = own[first + i, COLS - 1 : COLS, :]
    for n, (i, j) in enumerate(((0, 0), (0, COLS - 1), (ROWS - 1, 0), (ROWS - 1, COLS - 1))):
        corners[n] = jnp.broadcast_to(own[first + i, j : j + 1, :], corners.shape[1:])


def clear_outside(rows, strips):
    r, c = lax.axis_index("row"), lax.axis_index("col")

    @pl.when(r == 0)
    def _():
        rows[0] = jnp.zeros_like(rows[0])
        for side in range(2):
            strips[side, 0:8, :] = jnp.zeros_like(strips[side, 0:8, :])

    @pl.when(r == GRID_ROWS - 1)
    def _():
        rows[1] = jnp.zeros_like(rows[1])
        for side in range(2):
            strips[side, 32:40, :] = jnp.zeros_like(strips[side, 32:40, :])

    for side, edge in ((0, 0), (1, GRID_COLS - 1)):

        @pl.when(c == edge)
        def _():
            strips[side] = jnp.zeros_like(strips[side])


def reduce_kernel(
    features,
    cotangent,
    labels,
    taps_in,
    sums,
    mixed_pair,
    acts,
    fx,
    gx,
    lab,
    taps,
    fn,
    gn,
    fs,
    gs,
    f_ends,
    g_ends,
    f_corners,
    g_corners,
    lab_near,
    lab_square,
    mixed,
    mixed_t,
    rim_t,
    rim_acts,
    totals,
    parts,
    partner_part,
    chip_sum,
    landing,
    load,
    met,
    sems,
    got,
    f_send,
    f_recv,
    g_send,
    g_recv,
    l_send,
    l_recv,
):
    r, c = lax.axis_index("row"), lax.axis_index("col")
    x, y, z, k = place()
    me = x * 16 + y * 4 + z
    lines = (
        [at(x + d, y, z, k) for d in (1, 2, 3)],
        [at(x, y + d, z, k) for d in (1, 2, 3)],
        [at(x, y, z + d, k) for d in (1, 2, 3)],
    )
    partner = at(x, y, z, 1 - k)
    load_labels = pltpu.make_async_copy(labels, lab, load.at[0])
    load_taps = pltpu.make_async_copy(taps_in, taps, load.at[1])
    load_labels.start()
    load_taps.start()
    load_f = [
        pltpu.make_async_copy(
            features.at[pl.ds(8 * n, 8)], fx.at[pl.ds(1 + 8 * n, 8)], load.at[2 + n]
        )
        for n in range(3)
    ]
    load_g = [
        pltpu.make_async_copy(cotangent.at[pl.ds(8 * n, 8)], gx.at[pl.ds(8 * n, 8)], load.at[5 + n])
        for n in range(3)
    ]
    for copy in (*load_f, *load_g):
        copy.start()
    barrier = pltpu.get_barrier_semaphore()
    for device in [*lines[0], *lines[1], *lines[2], partner, *(beside(*side) for side in SIDES)]:
        signal(barrier, device)

    fx[0] = jnp.zeros_like(fx[0])
    fx[1 + ROWS] = jnp.zeros_like(fx[0])
    load_labels.wait()
    load_taps.wait()
    lab_square[0:ROWS, 0:COLS] = lab[...].astype(jnp.float32)
    by_column = lab_square[...].T
    for i in range(ROWS):
        acts[COLS * i : COLS * (i + 1), ONES] = onehot(by_column[0:COLS, i : i + 1], COLS)
    for copy in load_f:
        copy.wait()
    pack(fx, f_ends, f_corners, 1)
    f_copies = halo_copies(fx, fn, fs, f_ends, f_corners, f_send, f_recv, 1)
    g_copies = halo_copies(gx, gn, gs, g_ends, g_corners, g_send, g_recv, 0)
    l_copies = [
        remote(lab, lab_near.at[OPPOSITE[i]], l_send.at[i], l_recv.at[i], beside(*side))
        for i, side in enumerate(SIDES)
    ]
    tap = [taps[n // 3, n % 3 : n % 3 + 1] for n in range(9)]

    def mix(n):
        for i in range(8 * n, 8 * (n + 1)):
            above, here, below = fx[i], fx[i + 1], fx[i + 2]
            t = [tap[b] * above + tap[3 + b] * here + tap[6 + b] * below for b in range(3)]
            mixed[i] = here + t[1] + later(t[0]) + earlier(t[2])
        block = mixed[8 * n : 8 * (n + 1)].reshape(768, CHANS)
        for m in range(3):
            cell = slice(768 * n + 256 * m, 768 * n + 256 * (m + 1))
            mixed_t[0:256, cell], mixed_t[256:512, cell] = halves(
                block[256 * m : 256 * (m + 1)].T
            )

    def split(n):
        for i in range(8 * n, 8 * (n + 1)):
            cell = slice(COLS * i, COLS * (i + 1))
            acts[cell, UPPER], acts[cell, LOWER] = halves(gx[i])

    def add(which, n, value):
        totals[which] = value if n == 0 else totals[which] + value

    def sum_labels(n):
        cell = slice(768 * n, 768 * (n + 1))
        value = product(mixed_t[:, cell], acts[cell, ONES])
        add(0, n, value[0:256] + value[256:512])

    def sum_grads(n):
        cell = slice(768 * n, 768 * (n + 1))
        value = product(mixed_t[:, cell], acts[cell, UPPER])
        more = product(mixed_t[0:256, cell], acts[cell, LOWER])
        add(1, n, value[0:256] + value[256:512] + more)

    mix(0)
    sum_labels(0)
    mix(1)
    pl.semaphore_wait(barrier, 10 + len(SIDES))
    for copy in f_copies:
        copy.start()
    for device in lines[0]:
        signal(met.at[0], device)
    for copy in l_copies:
        copy.start()
    sum_labels(1)
    mix(2)
    for copy in load_g:
        copy.wait()
    pack(gx, g_ends, g_corners, 0)
    for copy in g_copies:
        copy.start()
    sum_labels(2)
    split(0)
    sum_grads(0)
    split(1)
    sum_grads(1)
    split(2)
    pl.semaphore_wait(met.at[0], 3)
    for device in lines[1]:
        signal(met.at[1], device)
    sum_grads(2)

    rim_acts[...] = jnp.zeros_like(rim_acts)
    rim_acts[0:COLS, :] = acts[0:COLS, :]
    rim_acts[COLS : 2 * COLS, :] = acts[CELLS - COLS : CELLS, :]
    fill = jnp.zeros((8, COUNT), jnp.float32)
    for side, column in ((0, 0), (1, COLS - 1)):
        cell = slice(192 + 32 * side, 224 + 32 * side)
        rim_acts[cell, UPPER], rim_acts[cell, LOWER] = halves(
            jnp.concatenate([g_ends[side], fill], axis=0)
        )
        rim_acts[cell, ONES] = onehot(lab_square[0:32, column : column + 1], 32)

    for copy in f_copies:
        copy.wait_recv()
    clear_outside(fn, fs)
    north = tap[1] * fn[0] + later(tap[0] * fn[0]) + earlier(tap[2] * fn[0])
    south = tap[7] * fn[1] + later(tap[6] * fn[1]) + earlier(tap[8] * fn[1])
    west = strip_sum(fs.at[0], [tap[3 * a] for a in range(3)])
    east = strip_sum(fs.at[1], [tap[3 * a + 2] for a in range(3)])
    gap = jnp.zeros((8, CHANS), jnp.float32)
    rim = jnp.concatenate([north, south, west, gap, east, gap], axis=0)
    rim_t[0:256, :], rim_t[256:512, :] = halves(rim.T)
    by_label = product(rim_t[...], rim_acts[:, ONES])
    parts[0] = (totals[0] + by_label[0:256] + by_label[256:512]).T.reshape(TILE)
    by_grad = product(rim_t[...], rim_acts[:, UPPER])
    by_grad = by_grad[0:256] + by_grad[256:512] + product(rim_t[0:256, :], rim_acts[:, LOWER])
    parts[1] = (totals[1] + by_grad).T.reshape(TILE)

    pair = remote(parts.at[1 - k], partner_part, sems.at[0], sems.at[1], partner)
    pair.start()
    pl.semaphore_wait(met.at[1], 3)
    pair.wait()
    chip_sum[...] = parts[k] + partner_part[...]

    for slot, code in enumerate(ORDER):
        device, chip = chip_at(code)
        remote(chip_sum.at[chip], landing.at[slot], sems.at[2], sems.at[3], device).start()

    mixed[0] = mixed[0] + north
    mixed[ROWS - 1] = mixed[ROWS - 1] + south
    for i in range(ROWS):
        mixed[i, 0:1, :] = mixed[i, 0:1, :] + west[i : i + 1]
        mixed[i, COLS - 1 : COLS, :] = mixed[i, COLS - 1 : COLS, :] + east[i : i + 1]

    def settle(i, _):
        cell = pl.ds(pl.multiple_of(i * COLS, COLS), COLS)
        mixed_pair[cell, 0:256], mixed_pair[cell, 256:512] = halves(mixed[i])

    lax.fori_loop(0, ROWS, settle, None)

    pltpu.make_async_copy(landing, landing, sems.at[3]).wait()
    sums[k, me] = chip_sum[me] + jnp.sum(landing[...], axis=0)

    for slot, code in enumerate(ORDER):
        device, _ = chip_at(code)
        remote(sums.at[k, me], sums.at[k, me], sems.at[4], got.at[(slot >= 42) + (slot >= 56)], device).start()

    for copy in (*g_copies, *l_copies):
        copy.wait_recv()
    clear_outside(gn, gs)
    for side in range(2):
        for start, value in ((NORTH + side * COLS, gn[side]), (WEST + side * STRIP, gs[side])):
            cell = slice(start, start + value.shape[0])
            acts[cell, UPPER], acts[cell, LOWER] = halves(value)
    near = [lab_near[i].astype(jnp.float32) for i in range(8)]
    lab_square[0:1, 0:COLS] = jnp.where(r > 0, near[0][ROWS - 1 : ROWS], -1.0)
    lab_square[1:2, 0:COLS] = jnp.where(r < GRID_ROWS - 1, near[1][0:1], -1.0)
    by_column = lab_square[...].T
    acts[NORTH : NORTH + COLS, ONES] = onehot(by_column[0:COLS, 0:1], COLS)
    acts[SOUTH : SOUTH + COLS, ONES] = onehot(by_column[0:COLS, 1:2], COLS)
    for side, column, inside in ((0, COLS - 1, c > 0), (1, 0, c < GRID_COLS - 1)):
        place_of = slice(column, column + 1)
        upper, beside_us, lower = near[4 + side], near[2 + side], near[6 + side]
        strip = jnp.concatenate(
            [
                jnp.where(
                    inside & (r > 0),
                    jnp.broadcast_to(upper[ROWS - 1 : ROWS, place_of], (8, 128)),
                    -1.0,
                ),
                jnp.where(inside, jnp.broadcast_to(beside_us[:, place_of], (ROWS, 128)), -1.0),
                jnp.where(
                    inside & (r < GRID_ROWS - 1),
                    jnp.broadcast_to(lower[0:1, place_of], (8, 128)),
                    -1.0,
                ),
                jnp.full((8, 128), -1.0, jnp.float32),
            ],
            axis=0,
        )
        cell = slice(WEST + side * STRIP, WEST + (side + 1) * STRIP)
        acts[cell, ONES] = onehot(strip[:, 0:1], STRIP)

    slab = sums.at[k, me]
    remote(slab, slab, sems.at[6], sems.at[7], partner).start()
    for group, (start, end) in enumerate(((0, 42), (42, 56), (56, 63))):
        block = landing.at[pl.ds(0, end - start)]
        pltpu.make_async_copy(block, block, got.at[group]).wait()
        for code in ORDER[start:end]:
            _, chip = chip_at(opposite(code))
            slab = sums.at[k, chip]
            remote(slab, slab, sems.at[6], sems.at[7], partner).start()
    pltpu.make_async_copy(landing, landing, sems.at[2]).wait()
    pltpu.make_async_copy(landing, landing, sems.at[4]).wait()
    for copy in (*f_copies, *g_copies, *l_copies):
        copy.wait_send()
    half = sums.at[k]
    remote(half, half, sems.at[6], sems.at[7], partner).wait()


def apply_kernel(
    sums,
    mixed_pair,
    acts,
    value_weight,
    key_weight,
    centers,
    gain,
    taps,
    new_centers,
    logits,
    grad_features,
    grad_centers,
    grad_value,
    grad_key,
    new_out,
    logits_out,
    features_out,
    centers_out,
    value_out,
    key_out,
    forth,
    back_pair,
    dm,
    ds,
    small,
    wide,
    grid,
):
    by_label, by_grad = sums[0].reshape(COUNT, CHANS), sums[1].reshape(COUNT, CHANS)
    totals = precise(by_label, value_weight[...])
    centers_out[...] = precise(by_grad, key_weight[...]) * SCALE
    centred = totals - jnp.mean(totals, axis=1, keepdims=True)
    inverse = lax.rsqrt(jnp.mean(centred * centred, axis=1, keepdims=True) + 1e-05)
    normed = centred * inverse
    new_out[...] = centers[...] + gain[...] * normed
    back = precise(new_out[...], key_weight[...], ((1,), (1,))) * SCALE
    back_high, back_low = halves(back)
    forth_high, forth_low = halves(back.T)
    forth[0:256, :] = forth_high
    forth[256:512, :] = forth_high
    forth[512:768, :] = forth_low
    dnorm = centers_out[...] * gain[...]
    dsums = inverse * (
        dnorm
        - jnp.mean(dnorm, axis=1, keepdims=True)
        - normed * jnp.mean(dnorm * normed, axis=1, keepdims=True)
    )
    spread = precise(dsums, value_weight[...], ((1,), (1,)))
    spread_high, spread_low = halves(spread)
    back_pair[0:512] = spread_high
    back_pair[512:1024] = back_high
    back_pair[1024:1536] = back_high
    back_pair[1536:2048] = spread_low
    back_pair[2048:2560] = back_low
    copies = []

    def send(out, to, sem):
        copies.append(pltpu.make_async_copy(out, to, sem))
        copies[-1].start()

    def project(n):
        cell = slice(384 * n, 384 * (n + 1))
        out = product(mixed_pair[cell, :], forth[0:512, :]) + product(
            mixed_pair[cell, 0:256], forth[512:768, :]
        )
        logits_out[4 * n : 4 * (n + 1)] = out.reshape(4, COLS, COUNT)

    def dmixed(start, size):
        cell = slice(start, start + size)
        return product(acts[cell, :], back_pair[0:1536, :]) + product(
            acts[cell, 0:1024], back_pair[1536:2560, :]
        )

    def spread_cells(n):
        dm[1 + 4 * n : 5 + 4 * n] = dmixed(384 * n, 384).reshape(4, COLS, CHANS)

    tap = [taps[2 - n // 3, 2 - n % 3 : 3 - n % 3] for n in range(9)]

    def unmix(n):
        for i in range(4 * n, 4 * (n + 1)):
            above, here, below = dm[i], dm[i + 1], dm[i + 2]
            t = [tap[b] * above + tap[3 + b] * here + tap[6 + b] * below for b in range(3)]
            west, east = west_rim[i : i + 1], east_rim[i : i + 1]
            features_out[i] = here + t[1] + later(t[0], west) + earlier(t[2], east)

    for n in range(6):
        project(n)
        if n % 2:
            rows = pl.ds(4 * (n - 1), 8)
            send(logits_out.at[rows], logits.at[rows], wide.at[n // 2])
    send(new_out, new_centers, small.at[0])
    send(centers_out, grad_centers, small.at[1])
    rim = dmixed(NORTH, FULL - CELLS)
    dm[0] = rim[0:COLS]
    dm[1 + ROWS] = rim[COLS : 2 * COLS]
    ds[0] = rim[2 * COLS : 2 * COLS + STRIP]
    ds[1] = rim[2 * COLS + STRIP :]
    west_rim = strip_sum(ds.at[0], [tap[3 * a] for a in range(3)])
    east_rim = strip_sum(ds.at[1], [tap[3 * a + 2] for a in range(3)])
    spread_cells(0)
    spread_cells(1)
    for n in range(6):
        unmix(n)
        if n < 4:
            spread_cells(n + 2)
        if n == 4:
            value_out[...] = precise(by_label, dsums, ((0,), (0,)))
            key_out[...] = precise(by_grad, new_out[...], ((0,), (0,))) * SCALE
            send(value_out, grad_value, small.at[2])
            send(key_out, grad_key, small.at[3])
        if n % 2:
            rows = pl.ds(4 * (n - 1), 8)
            send(features_out.at[rows], grad_features.at[rows], grid.at[n // 2])
    for copy in copies:
        copy.wait()


def shards(
    features, depth_kernel, value_weight, key_weight, centers, center_gain, labels, cotangent
):
    f32, b16, vm, dma = jnp.float32, jnp.bfloat16, pltpu.VMEM, pltpu.SemaphoreType.DMA
    features, cotangent, labels, taps = (
        pltpu.with_memory_space_constraint(value, pltpu.HBM)
        for value in (features, cotangent, labels, depth_kernel)
    )
    held = pl.pallas_call(
        reduce_kernel,
        out_shape=(
            vm((2, *TILE), f32),
            vm((CELLS, 2 * CHANS), b16),
            vm((FULL, 3 * COUNT), b16),
        ),
        in_specs=[OUTSIDE] * 4,
        out_specs=[WHOLE] * 3,
        scratch_shapes=[
            vm((2 + ROWS, COLS, CHANS), f32),
            vm((ROWS, COLS, COUNT), f32),
            vm((ROWS, COLS), jnp.int32),
            vm((3, 3, CHANS), f32),
            vm((2, COLS, CHANS), f32),
            vm((2, COLS, COUNT), f32),
            vm((2, STRIP, CHANS), f32),
            vm((2, STRIP, COUNT), f32),
            vm((2, ROWS, CHANS), f32),
            vm((2, ROWS, COUNT), f32),
            vm((4, 8, CHANS), f32),
            vm((4, 8, COUNT), f32),
            vm((8, ROWS, COLS), jnp.int32),
            vm((128, 128), f32),
            vm((ROWS, COLS, CHANS), f32),
            vm((2 * CHANS, CELLS), b16),
            vm((2 * CHANS, 256), b16),
            vm((256, 3 * COUNT), b16),
            vm((2, CHANS, COUNT), f32),
            vm((2, *TILE), f32),
            vm(TILE, f32),
            vm(TILE, f32),
            vm((63, 8, 256), f32),
            dma((8,)),
            pltpu.SemaphoreType.REGULAR((2,)),
            dma((8,)),
            dma((3,)),
            *[dma((8,))] * 6,
        ],
        compiler_params=pltpu.CompilerParams(
            collective_id=0, has_side_effects=True, vmem_limit_bytes=30 * 2**20
        ),
    )(features, cotangent, labels, taps)
    return pl.pallas_call(
        apply_kernel,
        out_shape=(
            jax.ShapeDtypeStruct((COUNT, CHANS), f32),
            jax.ShapeDtypeStruct((ROWS, COLS, COUNT), f32),
            jax.ShapeDtypeStruct((ROWS, COLS, CHANS), f32),
            jax.ShapeDtypeStruct((COUNT, CHANS), f32),
            jax.ShapeDtypeStruct((CHANS, CHANS), f32),
            jax.ShapeDtypeStruct((CHANS, CHANS), f32),
        ),
        in_specs=[WHOLE] * 8,
        out_specs=[OUTSIDE] * 6,
        scratch_shapes=[
            vm((COUNT, CHANS), f32),
            vm((ROWS, COLS, COUNT), f32),
            vm((ROWS, COLS, CHANS), f32),
            vm((COUNT, CHANS), f32),
            vm((CHANS, CHANS), f32),
            vm((CHANS, CHANS), f32),
            vm((768, COUNT), b16),
            vm((2560, CHANS), b16),
            vm((2 + ROWS, COLS, CHANS), f32),
            vm((2, STRIP, CHANS), f32),
            dma((4,)),
            dma((3,)),
            dma((3,)),
        ],
        compiler_params=pltpu.CompilerParams(vmem_limit_bytes=30 * 2**20),
    )(*held, value_weight, key_weight, centers, center_gain.reshape(1, CHANS), depth_kernel)


def solution(mesh):
    return jax.shard_map(
        shards,
        mesh=mesh,
        in_specs=(
            P("row", "col", None),
            P(),
            P(),
            P(),
            P(),
            P(),
            P("row", "col"),
            P("row", "col", None),
        ),
        out_specs=(P(), P("row", "col", None), P("row", "col", None), P(), P(), P()),
        check_vma=False,
    )
```
